256 devices in a mesh: seg: 16 (over y, x_lo, core), head: 16 (over z, x_hi).
Axes of the slice: x: 4 (x_hi: 2, x_lo: 2; x = x_hi * 2 + x_lo), y: 4, z: 8, core: 2. Of those that a mesh axis runs over, the one named last changes fastest.
Arguments:
- queries: bfloat16 [2048, 73728], P('seg', 'head')
- leaf_latent: bfloat16 [2048, 576], P('seg'), may hold values from -5 to 5
- ancestor_latent: bfloat16 [2048, 576], P('seg')
- ancestor_parent: int32 [16], replicated, may hold values from -1 to 14, as said below
- leaf_parent: int32 [16], P('seg'), may hold values from 7 to 15, as said below
- leaf_length: int32 [16], P('seg'), may hold values from 1 to 128
- value_up: bfloat16 [128, 512, 128], P('head'), may hold values from -0.25 to 0.25
- out_weight: bfloat16 [128, 128, 7168], P('head', 'seg'), may hold values from -0.0625 to 0.0625
Outputs:
- mixed: bfloat16 [2048, 7168], P('seg', 'head')
The draws below stay inside these ranges and needn't reach their ends.
Inputs may be any that keep to these rules, and one draw needn't show every extreme that they name: ancestor_parent[0] = -1; for 0 < i < 8 the parent is i - 1; beyond, the parent lies in [7, i - 1], and the last segment's parent is the one before it. `leaf_parent`: each leaf's parent is an ancestor segment of index 7 or more.
All inputs are finite; a program needn't handle non-finite values.
Results may differ from the reference program's by a relative error of at most 0.023.
Values may be sent and summed in bfloat16 or wider, within the bound.
No kernel may reach another device: no remote copies, remote signals or barrier semaphores. Data moves between devices by JAX's collectives and lax.ppermute only.
A program may use at most 128 MiB of HBM per device.

```python
import jax
import jax.numpy as jnp
from jax import lax

HEADS = 128
LATENT = 512
ROPE = 64
NOPE = 128
VHEAD = 128
D = 7168
SEG_LEN = 128
LEAVES = 16
ANC_SEGS = 16
TOKENS = 2048
ANC_TOKENS = 2048


def draw_ancestor_parent(key, part):
    key = jax.random.fold_in(key, 1)
    count = ANC_SEGS
    half = count // 2
    ids = jnp.arange(count, dtype=jnp.int32)
    upper = jnp.maximum(ids, half).astype(jnp.int32)
    pick = jax.random.randint(key, (count,), half - 1, upper).astype(jnp.int32)
    parents = jnp.where(ids < half, ids - 1, pick)
    parents = jnp.where(ids == count - 1, count - 2, parents)
    return parents.astype(jnp.int32)


def draw_leaf_parent(key, part):
    key = jax.random.fold_in(key, 2)
    pick = jax.random.randint(key, (LEAVES,), ANC_SEGS // 2 - 1, ANC_SEGS).astype(jnp.int32)
    pick = pick.at[0].set(ANC_SEGS - 1)
    pick = pick.at[1].set(ANC_SEGS // 2 - 1)
    return pick


def draw_leaf_length(key, part):
    key = jax.random.fold_in(key, 3)
    length = jax.random.randint(key, (LEAVES,), 1, SEG_LEN + 1).astype(jnp.int32)
    length = length.at[0].set(SEG_LEN)
    length = length.at[1].set(1)
    return length


def draw_ancestor_latent(key, part):
    key = jax.random.fold_in(key, 4)
    shape = (ANC_TOKENS, LATENT + ROPE)
    values = jnp.clip(jax.random.normal(key, shape, jnp.float32), -4.0, 4.0)
    return values.astype(jnp.bfloat16)


def draw_queries(key, part):
    key = jax.random.fold_in(key, 5)
    width = LATENT + ROPE
    shape = (TOKENS, HEADS, width)
    values = jnp.clip(jax.random.normal(key, shape, jnp.float32), -4.0, 4.0)
    return values.reshape(TOKENS, HEADS * width).astype(jnp.bfloat16)


def strengthened(drawn, own_key, source, target, shards_of, factor):
    def block_of(dim):
        return (jnp.arange(drawn.shape[dim]) // (drawn.shape[dim] // shards_of)).reshape((-1,) + (1,) * (drawn.ndim - 1 - dim))

    one_side = jax.random.permutation(own_key, shards_of)[block_of(target)]
    other_side = (block_of(target) + shards_of // 2) % shards_of
    return jnp.where((block_of(source) == one_side) | (block_of(source) == other_side), factor * drawn, drawn)


def levels(stream_key, shape, shards, low, top_value):
    loudness, own = 1.0, jax.random.fold_in(stream_key, 6)
    for dim, shards_of in shards:
        draws = jnp.exp(jax.random.uniform(jax.random.fold_in(own, dim), (shards_of,), jnp.float32, low / len(shards), top_value / len(shards)))
        loudness = loudness * jnp.repeat(draws, shape[dim] // shards_of).reshape([-1 if axis == dim else 1 for axis in range(len(shape))])
    return loudness


def scatter_about(stream_key, shape, deviation, reach, split=(), kind=jnp.bfloat16):
    array = deviation * jax.random.normal(stream_key, shape, jnp.float32)
    if split:
        array = array * levels(stream_key, shape, split, -0.22, 0.18)
    return jnp.clip(array, -reach, reach).astype(kind)


def bell_draw_with(rng, dims, spread, limit, split, heavy, kind=jnp.bfloat16):
    result = spread * jax.random.normal(rng, dims, jnp.float32)
    if split:
        result = result * levels(rng, dims, split, -0.22, 0.18)
    return jnp.clip(strengthened(result, jax.random.fold_in(rng, 3), *heavy), -limit, limit).astype(kind)


def setup_inputs(seed: int = 0) -> dict:
    streams_of = jax.random.split(jax.random.key(seed), 9)
    queries = draw_queries(jax.random.fold_in(streams_of[8], 71), 0)
    leaf_latent = scatter_about(streams_of[1], (TOKENS, LATENT + ROPE), 1.0, 5.0, ((0, 16),))
    ancestor_latent = draw_ancestor_latent(jax.random.fold_in(streams_of[8], 71), 0)
    ancestor_parent = draw_ancestor_parent(jax.random.fold_in(streams_of[8], 71), 0)
    leaf_parent = draw_leaf_parent(jax.random.fold_in(streams_of[8], 71), 0)
    leaf_length = draw_leaf_length(jax.random.fold_in(streams_of[8], 71), 0)
    value_up = scatter_about(streams_of[6], (HEADS, LATENT, VHEAD), LATENT ** -0.5, 0.25, ((0, 16),))
    out_weight = bell_draw_with(streams_of[7], (HEADS, VHEAD, D), (HEADS * VHEAD) ** -0.5, 0.0625, ((0, 16), (1, 16)), (0, 2, 16, 2.0))
    return dict(queries=queries, leaf_latent=leaf_latent, ancestor_latent=ancestor_latent, ancestor_parent=ancestor_parent, leaf_parent=leaf_parent, leaf_length=leaf_length, value_up=value_up, out_weight=out_weight)


NEG = -1e30


def chains(parents, start):
    count = parents.shape[0]
    ids = jnp.arange(count, dtype=jnp.int32)

    def advance(step, state):
        marked, current = state
        match = ids[None, :] == current[:, None]
        marked = marked | match
        nxt = jnp.sum(jnp.where(match, parents[None, :], 0), axis=1).astype(jnp.int32)
        current = jnp.where(current >= 0, nxt, -1).astype(jnp.int32)
        return marked, current

    marked = jnp.zeros((start.shape[0], count), dtype=bool)
    marked, current = lax.fori_loop(0, count, advance, (marked, start.astype(jnp.int32)))
    return marked


def reference(queries, leaf_latent, ancestor_latent, ancestor_parent, leaf_parent, leaf_length, value_up, out_weight):
    width = LATENT + ROPE
    scale = (NOPE + ROPE) ** -0.5
    used = chains(ancestor_parent, leaf_parent)
    query_all = queries.reshape(LEAVES, SEG_LEN, HEADS, width)
    own_all = leaf_latent.reshape(LEAVES, SEG_LEN, width)
    anc_f = ancestor_latent.astype(jnp.float32)
    anc_seg = jnp.arange(ANC_TOKENS, dtype=jnp.int32) // SEG_LEN
    pos = jnp.arange(SEG_LEN, dtype=jnp.int32)
    value_f = value_up.astype(jnp.float32)

    def one_leaf(items):
        query, own, mark, length = items
        qf = query.astype(jnp.float32)
        ownf = own.astype(jnp.float32)
        s_own = jnp.einsum('qhc,kc->hqk', qf, ownf) * scale
        keep_own = (pos[:, None] >= pos[None, :]) & (pos[None, :] < length)
        s_own = jnp.where(keep_own[None], s_own, NEG)
        s_anc = jnp.einsum('qhc,kc->hqk', qf, anc_f) * scale
        keep_anc = jnp.any((anc_seg[:, None] == jnp.arange(ANC_SEGS, dtype=jnp.int32)[None, :]) & mark[None, :], axis=1)
        s_anc = jnp.where(keep_anc[None, None, :], s_anc, NEG)
        scores = jnp.concatenate([s_own, s_anc], axis=2)
        top = jnp.max(scores, axis=2, keepdims=True)
        expo = jnp.exp(scores - top)
        total = jnp.sum(expo, axis=2)
        weight = expo.astype(jnp.bfloat16).astype(jnp.float32)
        values = jnp.concatenate([ownf[:, :LATENT], anc_f[:, :LATENT]], axis=0)
        latent_out = (jnp.einsum('hqk,kc->hqc', weight, values) / total[:, :, None]).astype(jnp.bfloat16)
        head_out = jnp.einsum('hqc,hcv->qhv', latent_out.astype(jnp.float32), value_f)
        head_out = jnp.where((pos < length)[:, None, None], head_out, 0.0)
        return head_out.astype(jnp.bfloat16)

    head_out = lax.map(one_leaf, (query_all, own_all, used, leaf_length))
    flat = head_out.reshape(TOKENS, HEADS * VHEAD)
    mixed = jnp.dot(flat, out_weight.reshape(HEADS * VHEAD, D), preferred_element_type=jnp.float32)
    return mixed.astype(jnp.bfloat16)
```

```python
import itertools

import jax
import jax.numpy as jnp
from jax import lax
from jax.experimental import pallas as pl
from jax.experimental.pallas import tpu as pltpu
from jax.sharding import PartitionSpec as P

LATENT = 512
ROPE = 64
WIDTH = LATENT + ROPE
NOPE = 128
SEG_LEN = 128
VHEAD = 128
HEADS_DEV = 8
ROWS = HEADS_DEV * SEG_LEN
ANC_SEGS = 16
COLS = 448

NEG = -1e30
LOG2E = 1.4426950408889634
SCALE = (NOPE + ROPE) ** -0.5


def seg_of(y, xl, c):
    return y * 4 + xl * 2 + c


def move(x, to):
    pairs = []
    for y, xl, c, z, xh in itertools.product(range(4), range(2), range(2), range(8), range(2)):
        ty, txl, tc, tz, txh = to(y, xl, c, z, xh)
        pairs.append((seg_of(y, xl, c) * 16 + z * 2 + xh, seg_of(ty, txl, tc) * 16 + tz * 2 + txh))
    return lax.ppermute(x, ("seg", "head"), pairs)


def swap_core(x):
    return move(x, lambda y, xl, c, z, xh: (y, xl, 1 - c, z, xh))


def swap_x(x, a, b):
    return move(x, lambda y, xl, c, z, xh: (y, xl ^ a, c, z, xh ^ b))


def from_y(x, r):
    return move(x, lambda y, xl, c, z, xh: ((y - r) % 4, xl, c, z, xh))


def to_z(x, k):
    return move(x, lambda y, xl, c, z, xh: (y, xl, c, (z + k) % 8, xh))


def to_owner(x):
    return move(x, lambda y, xl, c, z, xh: (y, z >> 2, (z >> 1) & 1, xl * 4 + c * 2 + xh, z & 1))


def attention_kernel(meta, q_ref, own_ref, *refs):
    anc_refs = refs[:8]
    up_ref, out_ref, keys, scores, top, total, accum, where_ref = refs[8:]
    y, xl, c = meta[18], meta[19], meta[20]
    length = meta[17]

    for slot in range(ANC_SEGS):
        where_ref[slot] = -1

    def walk(step, state):
        count, current = state
        valid = current >= 0

        @pl.when(valid)
        def _():
            rel_y = lax.bitwise_and((current >> 2) - y + 4, 3)
            rel_x = lax.bitwise_xor(lax.bitwise_and(current >> 1, 1), xl)
            rel_c = lax.bitwise_xor(lax.bitwise_and(current, 1), c)
            where_ref[rel_c * 8 + rel_y * 2 + rel_x] = count

        following = meta[jnp.maximum(current, 0)]
        return (jnp.where(valid, count + 1, count), jnp.where(valid, following, -1))

    end, _ = lax.fori_loop(0, ANC_SEGS, walk, (jnp.int32(1), meta[16]))

    keys[0] = own_ref[...]
    keys[end] = own_ref[...]
    for slot in range(ANC_SEGS):
        place = where_ref[slot]

        @pl.when(place >= 0)
        def _(slot=slot, place=place):
            keys[place] = anc_refs[slot // 2][slot % 2]

    pairs = (end + 1) // 2

    def score(j):
        pair = jnp.concatenate([keys[2 * j], keys[2 * j + 1]], axis=1)
        s = jnp.dot(q_ref[...], pair, preferred_element_type=jnp.float32)
        return s[:, :SEG_LEN], s[:, SEG_LEN:]

    row = lax.broadcasted_iota(jnp.int32, (ROWS, SEG_LEN), 0) & (SEG_LEN - 1)
    col = lax.broadcasted_iota(jnp.int32, (ROWS, SEG_LEN), 1)
    left, right = score(0)
    left = jnp.where((col <= row) & (col < length), left, NEG)
    scores[0, :, :SEG_LEN] = left
    scores[0, :, SEG_LEN:] = right
    top[...] = jnp.maximum(left, right)

    def first(j, carry):
        left, right = score(j)
        right = jnp.where(2 * j + 1 < end, right, NEG)
        scores[j, :, :SEG_LEN] = left
        scores[j, :, SEG_LEN:] = right
        top[...] = jnp.maximum(top[...], jnp.maximum(left, right))
        return carry

    lax.fori_loop(1, pairs, first, 0)
    factor = SCALE * LOG2E
    high = jnp.max(top[...], axis=1, keepdims=True)
    top[...] = jnp.broadcast_to(high, (ROWS, SEG_LEN))
    total[...] = jnp.zeros_like(total)
    accum[...] = jnp.zeros_like(accum)

    def second(j, carry):
        high = top[...]
        left = jnp.exp2((scores[j, :, :SEG_LEN] - high) * factor)
        right = jnp.exp2((scores[j, :, SEG_LEN:] - high) * factor)
        total[...] += left + right
        weight = jnp.concatenate([left, right], axis=1).astype(jnp.bfloat16)
        pair = jnp.concatenate([keys[2 * j, :LATENT], keys[2 * j + 1, :LATENT]], axis=1)
        accum[...] += lax.dot_general(
            weight, pair, (((1,), (1,)), ((), ())), preferred_element_type=jnp.float32
        )
        return carry

    lax.fori_loop(0, pairs, second, 0)
    pos = lax.broadcasted_iota(jnp.int32, (SEG_LEN, VHEAD), 0)
    for h in range(HEADS_DEV):
        rows = slice(h * SEG_LEN, (h + 1) * SEG_LEN)
        denominator = jnp.sum(total[rows], axis=1, keepdims=True)
        latent_out = (accum[rows] / denominator).astype(jnp.bfloat16)
        head_out = jnp.dot(latent_out, up_ref[h], preferred_element_type=jnp.float32)
        head_out = jnp.where(pos < length, head_out, 0.0).astype(jnp.bfloat16)
        for block in range(4):
            rel = lax.bitwise_and(block - y + 4, 3)
            out_ref[rel, :, h * 32 : (h + 1) * 32] = head_out[:, block * 32 : (block + 1) * 32]


def attention(meta, q, own, anc, up):
    vmem = pl.BlockSpec(memory_space=pltpu.VMEM)
    return pl.pallas_call(
        attention_kernel,
        out_shape=jax.ShapeDtypeStruct((4, SEG_LEN, 256), jnp.bfloat16),
        in_specs=[pl.BlockSpec(memory_space=pltpu.SMEM)] + [vmem] * 11,
        out_specs=vmem,
        scratch_shapes=[
            pltpu.VMEM((ANC_SEGS + 2, WIDTH, SEG_LEN), jnp.bfloat16),
            pltpu.VMEM((9, ROWS, 2 * SEG_LEN), jnp.float32),
            pltpu.VMEM((ROWS, SEG_LEN), jnp.float32),
            pltpu.VMEM((ROWS, SEG_LEN), jnp.float32),
            pltpu.VMEM((ROWS, LATENT), jnp.float32),
            pltpu.SMEM((ANC_SEGS,), jnp.int32),
        ],
        compiler_params=pltpu.CompilerParams(vmem_limit_bytes=48 * 2**20),
        cost_estimate=pl.CostEstimate(
            flops=4 * 10**9, bytes_accessed=6 * 2**20, transcendentals=2 * 10**6
        ),
        name="attention",
    )(meta, q, own, *anc, up)


def project_kernel(meta, *refs):
    heads = refs[:8]
    w0, w1, w3, w2a, w2b = refs[8:13]
    outs = refs[13:21]
    left, partial = refs[21:]
    xl, c, z = meta[19], meta[20], meta[21]
    weights = [[w0.at[0], w1.at[0], w2a, w3.at[0]], [w0.at[1], w1.at[1], w2b, w3.at[1]]]
    for b in range(2):
        for t in range(4):
            for r in range(4):
                left[t * SEG_LEN : (t + 1) * SEG_LEN, b * 1024 + r * 256 : b * 1024 + r * 256 + 256] = heads[t * 2 + b][r]
    for n in range(7):
        cols = slice(n * 128, (n + 1) * 128)
        value = None
        for b in range(2):
            for r in range(4):
                term = jnp.dot(
                    left[:, b * 1024 + r * 256 : b * 1024 + r * 256 + 256],
                    weights[b][r][:, cols],
                    preferred_element_type=jnp.float32,
                )
                value = term if value is None else value + term
        for t in range(4):
            partial[t, cols] = value[t * SEG_LEN : (t + 1) * SEG_LEN].T.astype(jnp.bfloat16)
    for k in range(8):
        target = lax.bitwise_and(z + k, 7)
        t = lax.bitwise_xor(target >> 2, xl) * 2 + lax.bitwise_xor(lax.bitwise_and(target >> 1, 1), c)
        half = lax.bitwise_and(target, 1)

        @pl.when(half == 0)
        def _(k=k, t=t):
            outs[k][...] = partial[t, :COLS]

        @pl.when(half == 1)
        def _(k=k, t=t):
            outs[k][...] = partial[t, COLS:]


def project(meta, heads, weights):
    vmem = pl.BlockSpec(memory_space=pltpu.VMEM)
    return pl.pallas_call(
        project_kernel,
        out_shape=[jax.ShapeDtypeStruct((COLS, SEG_LEN), jnp.bfloat16)] * 8,
        in_specs=[pl.BlockSpec(memory_space=pltpu.SMEM)] + [vmem] * 13,
        out_specs=[vmem] * 8,
        scratch_shapes=[
            pltpu.VMEM((4 * SEG_LEN, 2048), jnp.bfloat16),
            pltpu.VMEM((4, 2 * COLS, SEG_LEN), jnp.bfloat16),
        ],
        compiler_params=pltpu.CompilerParams(vmem_limit_bytes=48 * 2**20),
        cost_estimate=pl.CostEstimate(
            flops=2 * 10**9, bytes_accessed=8 * 2**20, transcendentals=0
        ),
        name="project",
    )(meta, *heads, *weights)


def per_device(
    queries,
    leaf_latent,
    ancestor_latent,
    ancestor_parent,
    leaf_parent,
    leaf_length,
    value_up,
    out_weight,
):
    seg, head = lax.axis_index("seg"), lax.axis_index("head")
    y, xl, c = seg // 4, (seg // 2) % 2, seg % 2
    z, xh = head // 2, head % 2
    place = jnp.stack([y, xl, c, z, xh]).astype(jnp.int32)
    meta = jnp.concatenate([ancestor_parent, leaf_parent, leaf_length, place])

    mine = ancestor_latent.T
    column = jnp.stack([mine, swap_x(mine, 1, 0)])
    anc = [column] + [from_y(column, r) for r in (1, 2, 3)]
    anc = anc + [swap_core(x) for x in anc]

    blocks = out_weight.reshape(HEADS_DEV, 8, 2, 2, 2, 2 * COLS).transpose(3, 2, 4, 0, 1, 5)
    keep = lax.dynamic_index_in_dim(blocks, c, 0, keepdims=False)
    other = swap_core(lax.dynamic_index_in_dim(blocks, 1 - c, 0, keepdims=False))
    cores = jnp.where(c == 0, jnp.stack([keep, other], 3), jnp.stack([other, keep], 3))

    def for_x(a, b):
        part = lax.dynamic_index_in_dim(cores, xl ^ a, 0, keepdims=False)
        part = lax.dynamic_index_in_dim(part, xh ^ b, 0, keepdims=False)
        return swap_x(part, a, b) if a or b else part

    rows = []
    for b in range(2):
        near, far = for_x(0, b), for_x(1, b)
        rows.append(jnp.where(xl == 0, jnp.stack([near, far], 1), jnp.stack([far, near], 1)))
    w0 = jnp.stack(rows).reshape(2, 256, 2 * COLS)
    w1, w3 = from_y(w0, 1), from_y(w0, 3)
    w2a, w2b = from_y(w1[0], 1), from_y(w3[1], 3)

    q = queries.reshape(SEG_LEN, HEADS_DEV, WIDTH).transpose(1, 0, 2).reshape(ROWS, WIDTH)
    head_out = attention(meta, q, leaf_latent.T, anc, value_up)

    heads = []
    for a in range(2):
        row = [head_out if not (a or b) else swap_x(head_out, a, b) for b in range(2)]
        heads += row + [swap_core(x) for x in row]
    parts = project(meta, heads, (w0, w1, w3, w2a, w2b))
    summed = parts[0].astype(jnp.float32)
    for k in range(1, 8):
        summed = summed + to_z(parts[k], k).astype(jnp.float32)
    return to_owner(summed.astype(jnp.bfloat16)).T


def solution(mesh):
    return jax.shard_map(
        per_device,
        mesh=mesh,
        in_specs=(
            P("seg", "head"),
            P("seg", None),
            P("seg", None),
            P(),
            P("seg"),
            P("seg"),
            P("head", None, None),
            P("head", "seg", None),
        ),
        out_specs=P("seg", "head"),
        check_vma=False,
    )
```

```python
import itertools

import jax
import jax.numpy as jnp
from jax import lax
from jax.experimental import pallas as pl
from jax.experimental.pallas import tpu as pltpu
from jax.sharding import PartitionSpec as P

LATENT = 512
ROPE = 64
WIDTH = LATENT + ROPE
NOPE = 128
SEG_LEN = 128
VHEAD = 128
HEADS_DEV = 8
ROWS = HEADS_DEV * SEG_LEN
ANC_SEGS = 16
COLS = 448
PAD = 64

NEG = -1e30
LOG2E = 1.4426950408889634
SCALE = (NOPE + ROPE) ** -0.5


def seg_of(y, xl, c):
    return y * 4 + xl * 2 + c


def move(x, to):
    pairs = []
    for y, xl, c, z, xh in itertools.product(range(4), range(2), range(2), range(8), range(2)):
        ty, txl, tc, tz, txh = to(y, xl, c, z, xh)
        pairs.append((seg_of(y, xl, c) * 16 + z * 2 + xh, seg_of(ty, txl, tc) * 16 + tz * 2 + txh))
    return lax.ppermute(x, ("seg", "head"), pairs)


def swap_core(x):
    return move(x, lambda y, xl, c, z, xh: (y, xl, 1 - c, z, xh))


def swap_x(x, a, b):
    return move(x, lambda y, xl, c, z, xh: (y, xl ^ a, c, z, xh ^ b))


def from_y(x, r):
    return move(x, lambda y, xl, c, z, xh: ((y - r) % 4, xl, c, z, xh))


def to_z(x, k):
    return move(x, lambda y, xl, c, z, xh: (y, xl, c, (z + k) % 8, xh))


def to_owner(x):
    return move(
        x, lambda y, xl, c, z, xh: (y, xl ^ (z >> 2), c ^ ((z >> 1) & 1), xl * 4 + c * 2 + xh, z & 1)
    )


def attention_kernel(meta, q_ref, own_ref, *refs):
    anc_refs = refs[:8]
    up_hbm, out_ref, keys, scores, top, total, accum, up_ref, where_ref, sems = refs[8:]
    y, xl, c = meta[18], meta[19], meta[20]
    length = meta[17]

    for slot in range(ANC_SEGS):
        where_ref[slot] = -1

    def walk(step, state):
        count, current = state
        valid = current >= 0

        @pl.when(valid)
        def _():
            rel_y = lax.bitwise_and((current >> 2) - y + 4, 3)
            rel_x = lax.bitwise_xor(lax.bitwise_and(current >> 1, 1), xl)
            rel_c = lax.bitwise_xor(lax.bitwise_and(current, 1), c)
            where_ref[rel_c * 8 + rel_y * 2 + rel_x] = count

        following = meta[jnp.maximum(current, 0)]
        return (jnp.where(valid, count + 1, count), jnp.where(valid, following, -1))

    end, _ = lax.fori_loop(0, ANC_SEGS, walk, (jnp.int32(1), meta[16]))

    body = pl.ds(PAD, WIDTH)
    copies = [
        (None, pltpu.make_async_copy(own_ref, keys.at[0, body], sems.at[ANC_SEGS])),
        (None, pltpu.make_async_copy(own_ref, keys.at[end, body], sems.at[ANC_SEGS + 1])),
    ]
    for slot in range(ANC_SEGS):
        place = where_ref[slot]
        target = keys.at[jnp.maximum(place, 0), body]
        source = anc_refs[slot // 2].at[slot % 2]
        copies.append((place >= 0, pltpu.make_async_copy(source, target, sems.at[slot])))
    for used, copy in copies:
        if used is None:
            copy.start()
        else:
            pl.when(used)(copy.start)
    up_copy = pltpu.make_async_copy(up_hbm, up_ref, sems.at[ANC_SEGS + 2])
    up_copy.start()
    keys[:, :PAD] = jnp.zeros((ANC_SEGS + 2, PAD, SEG_LEN), jnp.bfloat16)
    keys[:, PAD + WIDTH :] = jnp.zeros((ANC_SEGS + 2, PAD, SEG_LEN), jnp.bfloat16)
    for used, copy in copies:
        if used is None:
            copy.wait()
        else:
            pl.when(used)(copy.wait)

    pairs = (end + 1) // 2

    def queries(odd):
        starts = [h * WIDTH - PAD * odd for h in range(odd, HEADS_DEV, 2)]
        return jnp.concatenate([q_ref[:, s : s + WIDTH + PAD] for s in starts], axis=0)

    def score(j):
        pair = jnp.concatenate([keys[2 * j], keys[2 * j + 1]], axis=1)
        even = jnp.dot(queries(0), pair[PAD:], preferred_element_type=jnp.float32)
        odd = jnp.dot(queries(1), pair[: WIDTH + PAD], preferred_element_type=jnp.float32)
        s = jnp.concatenate([even, odd], axis=0)
        return s[:, :SEG_LEN], s[:, SEG_LEN:]

    row = lax.broadcasted_iota(jnp.int32, (ROWS, SEG_LEN), 0) & (SEG_LEN - 1)
    col = lax.broadcasted_iota(jnp.int32, (ROWS, SEG_LEN), 1)
    left, right = score(0)
    left = jnp.where((col <= row) & (col < length), left, NEG)
    scores[0, :, :SEG_LEN] = left
    scores[0, :, SEG_LEN:] = right
    top[...] = jnp.maximum(left, right)

    def first(j, carry):
        left, right = score(j)
        right = jnp.where(2 * j + 1 < end, right, NEG)
        scores[j, :, :SEG_LEN] = left
        scores[j, :, SEG_LEN:] = right
        top[...] = jnp.maximum(top[...], jnp.maximum(left, right))
        return carry

    lax.fori_loop(1, pairs, first, 0)
    factor = SCALE * LOG2E
    high = jnp.max(top[...], axis=1, keepdims=True)
    top[...] = jnp.broadcast_to(high, (ROWS, SEG_LEN))
    total[...] = jnp.zeros_like(total)
    accum[...] = jnp.zeros_like(accum)

    def second(j, carry):
        high = top[...]
        left = jnp.exp2((scores[j, :, :SEG_LEN] - high) * factor)
        right = jnp.exp2((scores[j, :, SEG_LEN:] - high) * factor)
        total[...] += left + right
        weight = jnp.concatenate([left, right], axis=1).astype(jnp.bfloat16)
        values = pl.ds(PAD, LATENT)
        pair = jnp.concatenate([keys[2 * j, values], keys[2 * j + 1, values]], axis=1)
        accum[...] += lax.dot_general(
            weight, pair, (((1,), (1,)), ((), ())), preferred_element_type=jnp.float32
        )
        return carry

    lax.fori_loop(0, pairs, second, 0)
    up_copy.wait()
    pos = lax.broadcasted_iota(jnp.int32, (SEG_LEN, VHEAD), 0)
    for h in range(HEADS_DEV):
        at = (h % 2) * (HEADS_DEV // 2) + h // 2
        rows = slice(at * SEG_LEN, (at + 1) * SEG_LEN)
        denominator = jnp.sum(total[rows], axis=1, keepdims=True)
        latent_out = (accum[rows] / denominator).astype(jnp.bfloat16)
        head_out = jnp.dot(latent_out, up_ref[h], preferred_element_type=jnp.float32)
        head_out = jnp.where(pos < length, head_out, 0.0).astype(jnp.bfloat16)
        for block in range(4):
            rel = lax.bitwise_and(block - y + 4, 3)
            out_ref[rel, :, h * 32 : (h + 1) * 32] = head_out[:, block * 32 : (block + 1) * 32]


def attention(meta, q, own, anc, up):
    vmem = pl.BlockSpec(memory_space=pltpu.VMEM)
    anywhere = pl.BlockSpec(memory_space=pl.ANY)
    return pl.pallas_call(
        attention_kernel,
        out_shape=jax.ShapeDtypeStruct((4, SEG_LEN, 256), jnp.bfloat16),
        in_specs=[pl.BlockSpec(memory_space=pltpu.SMEM), vmem] + [anywhere] * 10,
        out_specs=vmem,
        scratch_shapes=[
            pltpu.VMEM((ANC_SEGS + 2, WIDTH + 2 * PAD, SEG_LEN), jnp.bfloat16),
            pltpu.VMEM((9, ROWS, 2 * SEG_LEN), jnp.float32),
            pltpu.VMEM((ROWS, SEG_LEN), jnp.float32),
            pltpu.VMEM((ROWS, SEG_LEN), jnp.float32),
            pltpu.VMEM((ROWS, LATENT), jnp.float32),
            pltpu.VMEM((HEADS_DEV, LATENT, VHEAD), jnp.bfloat16),
            pltpu.SMEM((ANC_SEGS,), jnp.int32),
            pltpu.SemaphoreType.DMA((ANC_SEGS + 3,)),
        ],
        compiler_params=pltpu.CompilerParams(vmem_limit_bytes=30 * 2**20),
        cost_estimate=pl.CostEstimate(
            flops=4 * 10**9, bytes_accessed=6 * 2**20, transcendentals=2 * 10**6
        ),
        name="attention",
    )(meta, q, own, *anc, up)


def project_kernel(meta, *refs):
    heads = refs[:8]
    w0, w1, w3, w2a, w2b = refs[8:13]
    outs = refs[13:21]
    left, partial = refs[21:]
    z = meta[21]
    weights = [[w0.at[0], w1.at[0], w2a, w3.at[0]], [w0.at[1], w1.at[1], w2b, w3.at[1]]]
    for b in range(2):
        for t in range(4):
            for r in range(4):
                left[t * SEG_LEN : (t + 1) * SEG_LEN, b * 1024 + r * 256 : b * 1024 + r * 256 + 256] = heads[t * 2 + b][r]
    for n in range(7):
        cols = slice(n * 128, (n + 1) * 128)
        value = None
        for b in range(2):
            for r in range(4):
                term = jnp.dot(
                    left[:, b * 1024 + r * 256 : b * 1024 + r * 256 + 256],
                    weights[b][r][:, cols],
                    preferred_element_type=jnp.float32,
                )
                value = term if value is None else value + term
        for t in range(4):
            partial[t, cols] = value[t * SEG_LEN : (t + 1) * SEG_LEN].T.astype(jnp.bfloat16)
    for k in range(8):
        target = lax.bitwise_and(z + k, 7)
        t = target >> 1
        half = lax.bitwise_and(target, 1)

        @pl.when(half == 0)
        def _(k=k, t=t):
            outs[k][...] = partial[t, :COLS]

        @pl.when(half == 1)
        def _(k=k, t=t):
            outs[k][...] = partial[t, COLS:]


def project(meta, heads, weights):
    vmem = pl.BlockSpec(memory_space=pltpu.VMEM)
    return pl.pallas_call(
        project_kernel,
        out_shape=[jax.ShapeDtypeStruct((COLS, SEG_LEN), jnp.bfloat16)] * 8,
        in_specs=[pl.BlockSpec(memory_space=pltpu.SMEM)] + [vmem] * 13,
        out_specs=[vmem] * 8,
        scratch_shapes=[
            pltpu.VMEM((4 * SEG_LEN, 2048), jnp.bfloat16),
            pltpu.VMEM((4, 2 * COLS, SEG_LEN), jnp.bfloat16),
        ],
        compiler_params=pltpu.CompilerParams(vmem_limit_bytes=20 * 2**20),
        cost_estimate=pl.CostEstimate(
            flops=2 * 10**9, bytes_accessed=8 * 2**20, transcendentals=0
        ),
        name="project",
    )(meta, *heads, *weights)


def per_device(
    queries,
    leaf_latent,
    ancestor_latent,
    ancestor_parent,
    leaf_parent,
    leaf_length,
    value_up,
    out_weight,
):
    seg, head = lax.axis_index("seg"), lax.axis_index("head")
    y, xl, c = seg // 4, (seg // 2) % 2, seg % 2
    z, xh = head // 2, head % 2
    place = jnp.stack([y, xl, c, z, xh]).astype(jnp.int32)
    meta = jnp.concatenate([ancestor_parent, leaf_parent, leaf_length, place])

    mine = ancestor_latent.T
    column = jnp.stack([mine, swap_x(mine, 1, 0)])
    column, out_weight = lax.optimization_barrier((column, out_weight))

    blocks = out_weight.reshape(HEADS_DEV, 8, 2, 2, 2, 2 * COLS).transpose(3, 2, 4, 0, 1, 5)
    keep = lax.dynamic_index_in_dim(blocks, c, 0, keepdims=False)
    other = swap_core(lax.dynamic_index_in_dim(blocks, 1 - c, 0, keepdims=False))
    cores = jnp.where(c == 0, jnp.stack([keep, other], 3), jnp.stack([other, keep], 3))
    near, far = from_y(column, 1), from_y(column, 3)
    opposite = jnp.stack([from_y(near[0], 1), from_y(far[1], 3)])
    anc = [column, near, opposite, far]

    def for_x(a, b):
        part = lax.dynamic_index_in_dim(cores, xl ^ a, 0, keepdims=False)
        part = lax.dynamic_index_in_dim(part, xh ^ b, 0, keepdims=False)
        return swap_x(part, a, b) if a or b else part

    w0 = []
    for b in range(2):
        near, far = for_x(0, b), for_x(1, b)
        w0.append(jnp.where(xl == 0, jnp.stack([near, far], 1), jnp.stack([far, near], 1)))
    w0 = jnp.stack(w0).reshape(2, 256, 2 * COLS)
    w0, anc = lax.optimization_barrier((w0, anc))
    anc = anc + [swap_core(x) for x in anc]
    w1, w3 = from_y(w0, 1), from_y(w0, 3)
    w2a, w2b = from_y(w1[0], 1), from_y(w3[1], 3)

    head_out = attention(meta, queries, leaf_latent.T, anc, value_up)

    heads = []
    for a in range(2):
        row = [head_out if not (a or b) else swap_x(head_out, a, b) for b in range(2)]
        heads += row + [swap_core(x) for x in row]
    parts = project(meta, heads, (w0, w1, w3, w2a, w2b))
    summed = parts[0].astype(jnp.float32)
    for k in range(1, 8):
        summed = summed + to_z(parts[k], k).astype(jnp.float32)
    return to_owner(summed.astype(jnp.bfloat16)).T


def solution(mesh):
    return jax.shard_map(
        per_device,
        mesh=mesh,
        in_specs=(
            P("seg", "head"),
            P("seg", None),
            P("seg", None),
            P(),
            P("seg"),
            P("seg"),
            P("head", None, None),
            P("head", "seg", None),
        ),
        out_specs=P("seg", "head"),
        check_vma=False,
    )
```

```python
import itertools

import jax
import jax.numpy as jnp
from jax import lax
from jax.experimental import pallas as pl
from jax.experimental.pallas import tpu as pltpu
from jax.sharding import Mesh
from jax.sharding import PartitionSpec as P

LATENT = 512
ROPE = 64
WIDTH = LATENT + ROPE
NOPE = 128
SEG_LEN = 128
VHEAD = 128
HEADS_DEV = 8
ROWS = HEADS_DEV * SEG_LEN
ANC_SEGS = 16
COLS = 448
PAD = 64

NEAR = {0: (1, 0), 1: (1, 1), 7: (0, 0), 2: (0, 1)}

NEG = -1e30
LOG2E = 1.4426950408889634
SCALE = (NOPE + ROPE) ** -0.5


AXES = ("y", "xl", "c", "z", "xh")
SEG, HEAD = AXES[:3], AXES[3:]


def seg_of(y, xl, c):
    return y * 4 + xl * 2 + c


def move(x, to):
    pairs = []
    for y, xl, c, z, xh in itertools.product(range(4), range(2), range(2), range(8), range(2)):
        ty, txl, tc, tz, txh = to(y, xl, c, z, xh)
        pairs.append((seg_of(y, xl, c) * 16 + z * 2 + xh, seg_of(ty, txl, tc) * 16 + tz * 2 + txh))
    return lax.ppermute(x, AXES, pairs)


def swap_core(x):
    return move(x, lambda y, xl, c, z, xh: (y, xl, 1 - c, z, xh))


def swap_x(x, a, b):
    return move(x, lambda y, xl, c, z, xh: (y, xl ^ a, c, z, xh ^ b))


def from_y(x, r):
    return move(x, lambda y, xl, c, z, xh: ((y - r) % 4, xl, c, z, xh))


def to_z(x, k):
    return move(x, lambda y, xl, c, z, xh: (y, xl, c, (z + k) % 8, xh))


def to_owner(x, k):
    def to(y, xl, c, z, xh):
        for half in range(2):
            owner = xl * 2 + c + 4 * half
            step = (z + k - owner) % 8
            if step in NEAR:
                return (y, xl ^ NEAR[step][0], c ^ NEAR[step][1], owner, xh)

    return move(x, to)


def cut_kernel(meta, w_ref, keep_ref, other_ref):
    for c in range(2):

        @pl.when(meta[2] == c)
        def _(c=c):
            for core, ref in ((c, keep_ref), (1 - c, other_ref)):
                for xl in range(2):
                    for xh in range(2):
                        for half in range(2):
                            start = ((xl * 2 + core + 4 * half) * 2 + xh) * COLS
                            cols = slice(half * COLS, (half + 1) * COLS)
                            ref[xl, xh, :, :, cols] = w_ref[:, :, start : start + COLS]


def small_call(kernel, name, shapes, *args):
    vmem = pl.BlockSpec(memory_space=pltpu.VMEM)
    return pl.pallas_call(
        kernel,
        out_shape=[jax.ShapeDtypeStruct(x, jnp.bfloat16) for x in shapes],
        in_specs=[pl.BlockSpec(memory_space=pltpu.SMEM)] + [vmem] * (len(args) - 1),
        out_specs=[vmem] * len(shapes),
        cost_estimate=pl.CostEstimate(flops=0, bytes_accessed=2 * 2**20, transcendentals=0),
        name=name,
    )(*args)


def attention_kernel(meta, q_hbm, own_ref, *refs):
    anc_refs = refs[:8]
    up_hbm, out_ref, keys, scores, top, total, accum, up_ref, q_ref, mixed, where_ref, sems = refs[8:]
    y, xl, c = meta[18], meta[19], meta[20]
    length = meta[17]
    q_copy = pltpu.make_async_copy(q_hbm, q_ref, sems.at[0])
    q_copy.start()

    for slot in range(ANC_SEGS):
        where_ref[slot] = 0

    def walk(step, current):
        @pl.when(current >= 0)
        def _():
            rel_y = lax.bitwise_and((current >> 2) - y + 4, 3)
            rel_x = lax.bitwise_xor(lax.bitwise_and(current >> 1, 1), xl)
            rel_c = lax.bitwise_xor(lax.bitwise_and(current, 1), c)
            where_ref[rel_c * 8 + rel_y * 2 + rel_x] = 1

        return jnp.where(current >= 0, meta[jnp.maximum(current, 0)], -1)

    lax.fori_loop(0, ANC_SEGS, walk, meta[16])

    keys[0, PAD : PAD + WIDTH] = own_ref[...]
    end = jnp.int32(1)
    for slot in range(ANC_SEGS):
        used = where_ref[slot]

        @pl.when(used == 1)
        def _(slot=slot, place=end):
            keys[place, PAD : PAD + WIDTH] = anc_refs[slot // 2][slot % 2]

        end = end + used
    keys[end, PAD : PAD + WIDTH] = own_ref[...]

    up_copy = pltpu.make_async_copy(up_hbm, up_ref, sems.at[1])
    up_copy.start()
    keys[:, :PAD] = jnp.zeros((ANC_SEGS + 2, PAD, SEG_LEN), jnp.bfloat16)
    keys[:, PAD + WIDTH :] = jnp.zeros((ANC_SEGS + 2, PAD, SEG_LEN), jnp.bfloat16)
    q_copy.wait()
    pairs = (end + 1) // 2

    def queries(odd):
        starts = [h * WIDTH - PAD * odd for h in range(odd, HEADS_DEV, 2)]
        return jnp.concatenate([q_ref[:, s : s + WIDTH + PAD] for s in starts], axis=0)

    def score(j):
        pair = jnp.concatenate([keys[2 * j], keys[2 * j + 1]], axis=1)
        even = jnp.dot(queries(0), pair[PAD:], preferred_element_type=jnp.float32)
        odd = jnp.dot(queries(1), pair[: WIDTH + PAD], preferred_element_type=jnp.float32)
        s = jnp.concatenate([even, odd], axis=0)
        return s[:, :SEG_LEN], s[:, SEG_LEN:]

    row = lax.broadcasted_iota(jnp.int32, (ROWS, SEG_LEN), 0) & (SEG_LEN - 1)
    col = lax.broadcasted_iota(jnp.int32, (ROWS, SEG_LEN), 1)
    left, right = score(0)
    left = jnp.where((col <= row) & (col < length), left, NEG)
    scores[0, :, :SEG_LEN] = left
    scores[0, :, SEG_LEN:] = right
    top[...] = jnp.maximum(left, right)

    def first(j, carry):
        left, right = score(j)
        right = jnp.where(2 * j + 1 < end, right, NEG)
        scores[j, :, :SEG_LEN] = left
        scores[j, :, SEG_LEN:] = right
        top[...] = jnp.maximum(top[...], jnp.maximum(left, right))
        return carry

    lax.fori_loop(1, pairs, first, 0)
    factor = SCALE * LOG2E
    high = jnp.max(top[...], axis=1, keepdims=True)
    top[...] = jnp.broadcast_to(high, (ROWS, SEG_LEN))
    total[...] = jnp.zeros_like(total)
    accum[...] = jnp.zeros_like(accum)

    def second(j, carry):
        high = top[...]
        left = jnp.exp2((scores[j, :, :SEG_LEN] - high) * factor)
        right = jnp.exp2((scores[j, :, SEG_LEN:] - high) * factor)
        total[...] += left + right
        weight = jnp.concatenate([left, right], axis=1).astype(jnp.bfloat16)
        values = pl.ds(PAD, LATENT)
        pair = jnp.concatenate([keys[2 * j, values], keys[2 * j + 1, values]], axis=1)
        accum[...] += lax.dot_general(
            weight, pair, (((1,), (1,)), ((), ())), preferred_element_type=jnp.float32
        )
        return carry

    lax.fori_loop(0, pairs, second, 0)
    up_copy.wait()
    pos = lax.broadcasted_iota(jnp.int32, (SEG_LEN, VHEAD), 0)
    for h in range(HEADS_DEV):
        at = (h % 2) * (HEADS_DEV // 2) + h // 2
        rows = slice(at * SEG_LEN, (at + 1) * SEG_LEN)
        denominator = jnp.sum(total[rows], axis=1, keepdims=True)
        latent_out = (accum[rows] / denominator).astype(jnp.bfloat16)
        head_out = jnp.dot(latent_out, up_ref[h], preferred_element_type=jnp.float32)
        head_out = jnp.where(pos < length, head_out, 0.0).astype(jnp.bfloat16)
        for block in range(4):
            rel = lax.bitwise_and(block - y + 4, 3)
            mixed[rel, :, h * 32 : (h + 1) * 32] = head_out[:, block * 32 : (block + 1) * 32]
    for copy in range(4):
        out_ref[copy] = mixed[...]


def attention(meta, q, own, anc, up):
    vmem = pl.BlockSpec(memory_space=pltpu.VMEM)
    hbm = pl.BlockSpec(memory_space=pltpu.HBM)
    return pl.pallas_call(
        attention_kernel,
        out_shape=jax.ShapeDtypeStruct((4, 4, SEG_LEN, 256), jnp.bfloat16),
        in_specs=[pl.BlockSpec(memory_space=pltpu.SMEM), hbm] + [vmem] * 9 + [hbm],
        out_specs=vmem,
        scratch_shapes=[
            pltpu.VMEM((ANC_SEGS + 2, WIDTH + 2 * PAD, SEG_LEN), jnp.bfloat16),
            pltpu.VMEM((9, ROWS, 2 * SEG_LEN), jnp.float32),
            pltpu.VMEM((ROWS, SEG_LEN), jnp.float32),
            pltpu.VMEM((ROWS, SEG_LEN), jnp.float32),
            pltpu.VMEM((ROWS, LATENT), jnp.float32),
            pltpu.VMEM((HEADS_DEV, LATENT, VHEAD), jnp.bfloat16),
            pltpu.VMEM((SEG_LEN, HEADS_DEV * WIDTH), jnp.bfloat16),
            pltpu.VMEM((4, SEG_LEN, 256), jnp.bfloat16),
            pltpu.SMEM((ANC_SEGS,), jnp.int32),
            pltpu.SemaphoreType.DMA((2,)),
        ],
        compiler_params=pltpu.CompilerParams(vmem_limit_bytes=51 * 2**20),
        cost_estimate=pl.CostEstimate(
            flops=10**6, bytes_accessed=2**16, transcendentals=0
        ),
        name="attention",
    )(meta, q, own, *anc, up)


def project_kernel(meta, *refs):
    heads = refs[:2]
    w0, w1, w3, w2a, w2b = refs[2:7]
    outs = refs[7:13]
    left, partial = refs[13:]
    xl, c, z, xh = meta[19], meta[20], meta[21], meta[22]
    weights = [[w0.at[0], w1.at[0], w2a, w3.at[0]], [w0.at[1], w1.at[1], w2b, w3.at[1]]]
    for b in range(2):
        for t in range(4):
            source = lax.bitwise_xor(xl, t // 2) * 2 + lax.bitwise_xor(xh, b)
            for r in range(4):
                cols = slice(b * 1024 + r * 256, b * 1024 + r * 256 + 256)
                left[t * SEG_LEN : (t + 1) * SEG_LEN, cols] = heads[t % 2][source, r]
    for n in range(7):
        cols = slice(n * 128, (n + 1) * 128)
        value = None
        for b in range(2):
            for r in range(4):
                term = jnp.dot(
                    left[:, b * 1024 + r * 256 : b * 1024 + r * 256 + 256],
                    weights[b][r][:, cols],
                    preferred_element_type=jnp.float32,
                )
                value = term if value is None else value + term
        for t in range(4):
            partial[t, cols] = value[t * SEG_LEN : (t + 1) * SEG_LEN].T.astype(jnp.bfloat16)
    places = {0: (0, None), 1: (1, 0), 3: (1, 1), 7: (2, 0), 5: (2, 1), 4: (3, None), 2: (4, None), 6: (5, None)}
    for k, (out, part) in places.items():
        step = lax.bitwise_and(z + k - xl * 2 - c, 7)
        upper = (step >= 3) & (step <= 6)
        near = lax.bitwise_and(jnp.where(upper, step - 4, step), 7)
        t = sum(jnp.where(near == n, a * 2 + d, 0) for n, (a, d) in NEAR.items())
        ref = outs[out] if part is None else outs[out].at[part]

        @pl.when(jnp.logical_not(upper))
        def _(ref=ref, t=t):
            ref[...] = partial[t, :COLS]

        @pl.when(upper)
        def _(ref=ref, t=t):
            ref[...] = partial[t, COLS:]


def project(meta, heads, weights):
    vmem = pl.BlockSpec(memory_space=pltpu.VMEM)
    one = jax.ShapeDtypeStruct((COLS, SEG_LEN), jnp.bfloat16)
    two = jax.ShapeDtypeStruct((2, COLS, SEG_LEN), jnp.bfloat16)
    return pl.pallas_call(
        project_kernel,
        out_shape=[one, two, two, one, one, one],
        in_specs=[pl.BlockSpec(memory_space=pltpu.SMEM)] + [vmem] * 7,
        out_specs=[vmem] * 6,
        scratch_shapes=[
            pltpu.VMEM((4 * SEG_LEN, 2048), jnp.bfloat16),
            pltpu.VMEM((4, 2 * COLS, SEG_LEN), jnp.bfloat16),
        ],
        compiler_params=pltpu.CompilerParams(vmem_limit_bytes=20 * 2**20),
        cost_estimate=pl.CostEstimate(
            flops=10**6, bytes_accessed=2**16, transcendentals=0
        ),
        name="project",
    )(meta, *heads, *weights)


def per_device(
    queries,
    leaf_latent,
    ancestor_latent,
    ancestor_parent,
    leaf_parent,
    leaf_length,
    value_up,
    out_weight,
):
    y, xl, c, z, xh = [lax.axis_index(name) for name in AXES]
    place = jnp.stack([y, xl, c, z, xh]).astype(jnp.int32)
    meta = jnp.concatenate([ancestor_parent, leaf_parent, leaf_length, place])

    mine = ancestor_latent.T
    column = jnp.stack([mine, swap_x(mine, 1, 0)])

    keep, other = small_call(cut_kernel, "cut", [(2, 2, HEADS_DEV, 8, 2 * COLS)] * 2, place, out_weight)
    other = swap_core(other)
    cores = jnp.where(c == 0, jnp.stack([keep, other], 3), jnp.stack([other, keep], 3))

    def for_x(a, b):
        part = lax.dynamic_index_in_dim(cores, xl ^ a, 0, keepdims=False)
        return lax.dynamic_index_in_dim(part, xh ^ b, 0, keepdims=False)

    w00, w10, w11 = for_x(0, 0), swap_x(for_x(1, 0), 1, 0), swap_x(for_x(1, 1), 1, 1)
    w01, _ = lax.optimization_barrier((for_x(0, 1), w10))
    w01 = swap_x(w01, 0, 1)
    anc = [column] + [from_y(column, r) for r in (1, 2, 3)]
    w0, _ = lax.optimization_barrier(([[w00, w01], [w10, w11]], anc))
    anc = anc + [swap_core(x) for x in anc]

    w0 = [jnp.stack(x) for x in w0]
    w0 = jnp.where(xl == 0, jnp.stack(w0, 2), jnp.stack(w0[::-1], 2)).reshape(2, 256, 2 * COLS)
    w1, w3 = from_y(w0, 1), from_y(w0, 3)
    w2a, w2b = w1[0], w3[1]

    head_out = attention(meta, queries, leaf_latent.T, anc, value_up)

    w2a, w2b, _ = lax.optimization_barrier((w2a, w2b, head_out))
    w2a, w2b = from_y(w2a, 1), from_y(w2b, 3)
    heads = lax.all_to_all(head_out, ("xl", "xh"), 0, 0)
    heads, w2a, w2b = lax.optimization_barrier((heads, w2a, w2b))
    heads = (heads, swap_core(heads))
    mine, right, left, far, right2, left2 = project(meta, heads, (w0, w1, w3, w2a, w2b))
    right, left = to_z(right, 1), to_z(left, -1)
    far = move(far, lambda y, xl, c, z, xh: (y, xl, c, (z + 2 - 4 * c) % 8, xh))

    def f32(x):
        return x.astype(jnp.float32)

    mine = f32(mine) + f32(right[0]) + f32(left[0])
    right2 = f32(right2) + f32(right[1]) + jnp.where(c == 0, f32(far), 0.0)
    left2 = f32(left2) + f32(left[1]) + jnp.where(c == 1, f32(far), 0.0)
    terms = [to_owner(x.astype(jnp.bfloat16), k) for x, k in ((mine, 0), (right2, 2), (left2, -2))]
    return (f32(terms[0]) + f32(terms[1]) + f32(terms[2])).astype(jnp.bfloat16).T


def solution(mesh):
    mesh = Mesh(mesh.devices.reshape(4, 2, 2, 8, 2), AXES)
    return jax.shard_map(
        per_device,
        mesh=mesh,
        in_specs=(
            P(SEG, HEAD),
            P(SEG, None),
            P(SEG, None),
            P(),
            P(SEG),
            P(SEG),
            P(HEAD, None, None),
            P(HEAD, SEG, None),
        ),
        out_specs=P(SEG, HEAD),
        check_vma=False,
    )
```

```python
import itertools

import jax
import jax.numpy as jnp
from jax import lax
from jax.experimental import pallas as pl
from jax.experimental.pallas import tpu as pltpu
from jax.sharding import Mesh
from jax.sharding import PartitionSpec as P

LATENT = 512
ROPE = 64
WIDTH = LATENT + ROPE
NOPE = 128
SEG_LEN = 128
VHEAD = 128
HEADS_DEV = 8
ROWS = HEADS_DEV * SEG_LEN
ANC_SEGS = 16
COLS = 448
PAD = 64

NEAR = {0: (1, 0), 1: (1, 1), 7: (0, 0), 2: (0, 1)}

NEG = -1e30
LOG2E = 1.4426950408889634
SCALE = (NOPE + ROPE) ** -0.5


AXES = ("y", "xl", "c", "z", "xh")
SEG, HEAD = AXES[:3], AXES[3:]


def seg_of(y, xl, c):
    return y * 4 + xl * 2 + c


def move(x, to):
    pairs = []
    for y, xl, c, z, xh in itertools.product(range(4), range(2), range(2), range(8), range(2)):
        ty, txl, tc, tz, txh = to(y, xl, c, z, xh)
        pairs.append((seg_of(y, xl, c) * 16 + z * 2 + xh, seg_of(ty, txl, tc) * 16 + tz * 2 + txh))
    return lax.ppermute(x, AXES, pairs)


def swap_core(x):
    return move(x, lambda y, xl, c, z, xh: (y, xl, 1 - c, z, xh))


def swap_x(x, a, b):
    return move(x, lambda y, xl, c, z, xh: (y, xl ^ a, c, z, xh ^ b))


def from_y(x, r):
    return move(x, lambda y, xl, c, z, xh: ((y - r) % 4, xl, c, z, xh))


def to_z(x, k):
    return move(x, lambda y, xl, c, z, xh: (y, xl, c, (z + k) % 8, xh))


def to_owner(x, k):
    def to(y, xl, c, z, xh):
        for half in range(2):
            owner = xl * 2 + c + 4 * half
            step = (z + k - owner) * (1 - 2 * c) % 8
            if step in NEAR:
                return (y, xl ^ NEAR[step][0], c ^ NEAR[step][1], owner, xh)

    return move(x, to)


def cut_kernel(meta, w_ref, keep_ref, other_ref):
    for c in range(2):

        @pl.when(meta[2] == c)
        def _(c=c):
            for core, ref in ((c, keep_ref), (1 - c, other_ref)):
                for xl in range(2):
                    for xh in range(2):
                        for half in range(2):
                            start = ((xl * 2 + core + 4 * half) * 2 + xh) * COLS
                            cols = slice(half * COLS, (half + 1) * COLS)
                            ref[xl, xh, :, :, cols] = w_ref[:, :, start : start + COLS]


def small_call(kernel, name, shapes, *args):
    vmem = pl.BlockSpec(memory_space=pltpu.VMEM)
    return pl.pallas_call(
        kernel,
        out_shape=[jax.ShapeDtypeStruct(x, jnp.bfloat16) for x in shapes],
        in_specs=[pl.BlockSpec(memory_space=pltpu.SMEM)] + [vmem] * (len(args) - 1),
        out_specs=[vmem] * len(shapes),
        compiler_params=pltpu.CompilerParams(vmem_limit_bytes=12 * 2**20),
        cost_estimate=pl.CostEstimate(flops=0, bytes_accessed=2 * 2**20, transcendentals=0),
        name=name,
    )(*args)


def attention_kernel(meta, q_hbm, own_ref, *refs):
    anc_refs = refs[:8]
    up_hbm, out_ref, keys, scores, top, total, accum, up_ref, q_ref, mixed, where_ref, sems = refs[8:]
    y, xl, c = meta[18], meta[19], meta[20]
    length = meta[17]
    q_copy = pltpu.make_async_copy(q_hbm, q_ref, sems.at[0])
    q_copy.start()

    for slot in range(ANC_SEGS):
        where_ref[slot] = 0

    def walk(step, current):
        @pl.when(current >= 0)
        def _():
            rel_y = lax.bitwise_and((current >> 2) - y + 4, 3)
            rel_x = lax.bitwise_xor(lax.bitwise_and(current >> 1, 1), xl)
            rel_c = lax.bitwise_xor(lax.bitwise_and(current, 1), c)
            where_ref[rel_c * 8 + rel_y * 2 + rel_x] = 1

        return jnp.where(current >= 0, meta[jnp.maximum(current, 0)], -1)

    lax.fori_loop(0, ANC_SEGS, walk, meta[16])

    keys[0, PAD : PAD + WIDTH] = own_ref[...]
    end = jnp.int32(1)
    for slot in range(ANC_SEGS):
        used = where_ref[slot]

        @pl.when(used == 1)
        def _(slot=slot, place=end):
            keys[place, PAD : PAD + WIDTH] = anc_refs[slot // 2][slot % 2]

        end = end + used
    keys[end, PAD : PAD + WIDTH] = own_ref[...]

    up_copy = pltpu.make_async_copy(up_hbm, up_ref, sems.at[1])
    up_copy.start()
    keys[:, :PAD] = jnp.zeros((ANC_SEGS + 2, PAD, SEG_LEN), jnp.bfloat16)
    keys[:, PAD + WIDTH :] = jnp.zeros((ANC_SEGS + 2, PAD, SEG_LEN), jnp.bfloat16)
    q_copy.wait()
    pairs = (end + 1) // 2

    def queries(odd):
        starts = [h * WIDTH - PAD * odd for h in range(odd, HEADS_DEV, 2)]
        return jnp.concatenate([q_ref[:, s : s + WIDTH + PAD] for s in starts], axis=0)

    def score(j):
        pair = jnp.concatenate([keys[2 * j], keys[2 * j + 1]], axis=1)
        even = jnp.dot(queries(0), pair[PAD:], preferred_element_type=jnp.float32)
        odd = jnp.dot(queries(1), pair[: WIDTH + PAD], preferred_element_type=jnp.float32)
        s = jnp.concatenate([even, odd], axis=0)
        return s[:, :SEG_LEN], s[:, SEG_LEN:]

    row = lax.broadcasted_iota(jnp.int32, (ROWS, SEG_LEN), 0) & (SEG_LEN - 1)
    col = lax.broadcasted_iota(jnp.int32, (ROWS, SEG_LEN), 1)
    left, right = score(0)
    left = jnp.where((col <= row) & (col < length), left, NEG)
    scores[0, :, :SEG_LEN] = left
    scores[0, :, SEG_LEN:] = right
    top[...] = jnp.maximum(left, right)

    def first(j, carry):
        left, right = score(j)
        right = jnp.where(2 * j + 1 < end, right, NEG)
        scores[j, :, :SEG_LEN] = left
        scores[j, :, SEG_LEN:] = right
        top[...] = jnp.maximum(top[...], jnp.maximum(left, right))
        return carry

    lax.fori_loop(1, pairs, first, 0)
    factor = SCALE * LOG2E
    high = jnp.max(top[...], axis=1, keepdims=True)
    top[...] = jnp.broadcast_to(high, (ROWS, SEG_LEN))
    total[...] = jnp.zeros_like(total)
    accum[...] = jnp.zeros_like(accum)

    def second(j, carry):
        high = top[...]
        left = jnp.exp2((scores[j, :, :SEG_LEN] - high) * factor)
        right = jnp.exp2((scores[j, :, SEG_LEN:] - high) * factor)
        total[...] += left + right
        weight = jnp.concatenate([left, right], axis=1).astype(jnp.bfloat16)
        values = pl.ds(PAD, LATENT)
        pair = jnp.concatenate([keys[2 * j, values], keys[2 * j + 1, values]], axis=1)
        accum[...] += lax.dot_general(
            weight, pair, (((1,), (1,)), ((), ())), preferred_element_type=jnp.float32
        )
        return carry

    lax.fori_loop(0, pairs, second, 0)
    up_copy.wait()
    pos = lax.broadcasted_iota(jnp.int32, (SEG_LEN, VHEAD), 0)
    for h in range(HEADS_DEV):
        at = (h % 2) * (HEADS_DEV // 2) + h // 2
        rows = slice(at * SEG_LEN, (at + 1) * SEG_LEN)
        denominator = jnp.sum(total[rows], axis=1, keepdims=True)
        latent_out = (accum[rows] / denominator).astype(jnp.bfloat16)
        head_out = jnp.dot(latent_out, up_ref[h], preferred_element_type=jnp.float32)
        head_out = jnp.where(pos < length, head_out, 0.0).astype(jnp.bfloat16)
        for block in range(4):
            rel = lax.bitwise_and(block - y + 4, 3)
            mixed[rel, :, h * 32 : (h + 1) * 32] = head_out[:, block * 32 : (block + 1) * 32]
    for copy in range(4):
        out_ref[copy] = mixed[...]


def attention(meta, q, own, anc, up):
    vmem = pl.BlockSpec(memory_space=pltpu.VMEM)
    hbm = pl.BlockSpec(memory_space=pltpu.HBM)
    return pl.pallas_call(
        attention_kernel,
        out_shape=jax.ShapeDtypeStruct((4, 4, SEG_LEN, 256), jnp.bfloat16),
        in_specs=[pl.BlockSpec(memory_space=pltpu.SMEM), hbm] + [vmem] * 9 + [hbm],
        out_specs=vmem,
        scratch_shapes=[
            pltpu.VMEM((ANC_SEGS + 2, WIDTH + 2 * PAD, SEG_LEN), jnp.bfloat16),
            pltpu.VMEM((9, ROWS, 2 * SEG_LEN), jnp.float32),
            pltpu.VMEM((ROWS, SEG_LEN), jnp.float32),
            pltpu.VMEM((ROWS, SEG_LEN), jnp.float32),
            pltpu.VMEM((ROWS, LATENT), jnp.float32),
            pltpu.VMEM((HEADS_DEV, LATENT, VHEAD), jnp.bfloat16),
            pltpu.VMEM((SEG_LEN, HEADS_DEV * WIDTH), jnp.bfloat16),
            pltpu.VMEM((4, SEG_LEN, 256), jnp.bfloat16),
            pltpu.SMEM((ANC_SEGS,), jnp.int32),
            pltpu.SemaphoreType.DMA((2,)),
        ],
        compiler_params=pltpu.CompilerParams(vmem_limit_bytes=51 * 2**20),
        cost_estimate=pl.CostEstimate(
            flops=10**6, bytes_accessed=2**16, transcendentals=0
        ),
        name="attention",
    )(meta, q, own, *anc, up)


def project_kernel(meta, *refs):
    heads = refs[:2]
    w0, w1, w3, w2a, w2b = refs[2:7]
    outs = refs[7:13]
    left, partial = refs[13:]
    xl, c, z, xh = meta[19], meta[20], meta[21], meta[22]
    weights = [[w0.at[0], w1.at[0], w2a, w3.at[0]], [w0.at[1], w1.at[1], w2b, w3.at[1]]]
    for b in range(2):
        for t in range(4):
            source = lax.bitwise_xor(xl, t // 2) * 2 + lax.bitwise_xor(xh, b)
            for r in range(4):
                cols = slice(b * 1024 + r * 256, b * 1024 + r * 256 + 256)
                left[t * SEG_LEN : (t + 1) * SEG_LEN, cols] = heads[t % 2][source, r]
    for start in range(0, 896, 256):
        width = min(256, 896 - start)
        cols = slice(start, start + width)
        right = jnp.concatenate([weights[b][r][:, cols] for b in range(2) for r in range(4)], axis=0)
        value = jnp.dot(left[...], right, preferred_element_type=jnp.float32)
        for t in range(4):
            partial[t, cols] = value[t * SEG_LEN : (t + 1) * SEG_LEN].T.astype(jnp.bfloat16)
    places = {0: (0, None), 1: (1, 0), 3: (1, 1), 7: (2, 0), 5: (2, 1), 4: (3, None), 2: (4, None), 6: (5, None)}
    for k, (out, part) in places.items():
        step = lax.bitwise_and((z + k - xl * 2 - c) * (1 - 2 * c), 7)
        upper = (step >= 3) & (step <= 6)
        near = lax.bitwise_and(jnp.where(upper, step - 4, step), 7)
        t = sum(jnp.where(near == n, a * 2 + d, 0) for n, (a, d) in NEAR.items())
        ref = outs[out] if part is None else outs[out].at[part]

        @pl.when(jnp.logical_not(upper))
        def _(ref=ref, t=t):
            ref[...] = partial[t, :COLS]

        @pl.when(upper)
        def _(ref=ref, t=t):
            ref[...] = partial[t, COLS:]


def project(meta, heads, weights):
    vmem = pl.BlockSpec(memory_space=pltpu.VMEM)
    one = jax.ShapeDtypeStruct((COLS, SEG_LEN), jnp.bfloat16)
    two = jax.ShapeDtypeStruct((2, COLS, SEG_LEN), jnp.bfloat16)
    return pl.pallas_call(
        project_kernel,
        out_shape=[one, two, two, one, one, one],
        in_specs=[pl.BlockSpec(memory_space=pltpu.SMEM)] + [vmem] * 7,
        out_specs=[vmem] * 6,
        scratch_shapes=[
            pltpu.VMEM((4 * SEG_LEN, 2048), jnp.bfloat16),
            pltpu.VMEM((4, 2 * COLS, SEG_LEN), jnp.bfloat16),
        ],
        compiler_params=pltpu.CompilerParams(vmem_limit_bytes=20 * 2**20),
        cost_estimate=pl.CostEstimate(
            flops=10**6, bytes_accessed=2**16, transcendentals=0
        ),
        name="project",
    )(meta, *heads, *weights)


def per_device(
    queries,
    leaf_latent,
    ancestor_latent,
    ancestor_parent,
    leaf_parent,
    leaf_length,
    value_up,
    out_weight,
):
    y, xl, c, z, xh = [lax.axis_index(name) for name in AXES]
    place = jnp.stack([y, xl, c, z, xh]).astype(jnp.int32)
    meta = jnp.concatenate([ancestor_parent, leaf_parent, leaf_length, place])

    mine = ancestor_latent.T
    column = jnp.stack([mine, swap_x(mine, 1, 0)])

    keep, other = small_call(cut_kernel, "cut", [(2, 2, HEADS_DEV, 8, 2 * COLS)] * 2, place, out_weight)
    other = swap_core(other)
    cores = jnp.where(c == 0, jnp.stack([keep, other], 3), jnp.stack([other, keep], 3))

    def for_x(a, b):
        part = lax.dynamic_index_in_dim(cores, xl ^ a, 0, keepdims=False)
        return lax.dynamic_index_in_dim(part, xh ^ b, 0, keepdims=False)

    w00, w10, w11 = for_x(0, 0), swap_x(for_x(1, 0), 1, 0), swap_x(for_x(1, 1), 1, 1)
    w01, _ = lax.optimization_barrier((for_x(0, 1), w10))
    w01 = swap_x(w01, 0, 1)
    anc = [column] + [from_y(column, r) for r in (1, 2, 3)]
    w0, _ = lax.optimization_barrier(([[w00, w01], [w10, w11]], anc))
    anc = anc + [swap_core(x) for x in anc]

    w0 = [jnp.stack(x) for x in w0]
    w0 = jnp.where(xl == 0, jnp.stack(w0, 2), jnp.stack(w0[::-1], 2)).reshape(2, 256, 2 * COLS)
    w1, w3 = from_y(w0, 1), from_y(w0, 3)
    w2a, w2b = w1[0], w3[1]

    head_out = attention(meta, queries, leaf_latent.T, anc, value_up)

    w2a, w2b, _ = lax.optimization_barrier((w2a, w2b, head_out))
    w2a, w2b = from_y(w2a, 1), from_y(w2b, 3)
    heads = lax.all_to_all(head_out, ("xl", "xh"), 0, 0)
    heads, w2a, w2b = lax.optimization_barrier((heads, w2a, w2b))
    heads = (heads, swap_core(heads))
    mine, right, left, far, right2, left2 = project(meta, heads, (w0, w1, w3, w2a, w2b))
    right, left = to_z(right, 1), to_z(left, -1)
    far = move(far, lambda y, xl, c, z, xh: (y, xl, c, (z + 2 - 4 * c) % 8, xh))

    def f32(x):
        return x.astype(jnp.float32)

    mine = f32(mine) + f32(right[0]) + f32(left[0])
    right2 = f32(right2) + f32(right[1]) + jnp.where(c == 0, f32(far), 0.0)
    left2 = f32(left2) + f32(left[1]) + jnp.where(c == 1, f32(far), 0.0)
    terms = [to_owner(x.astype(jnp.bfloat16), k) for x, k in ((mine, 0), (right2, 2), (left2, -2))]
    return (f32(terms[0]) + f32(terms[1]) + f32(terms[2])).astype(jnp.bfloat16).T


def solution(mesh):
    mesh = Mesh(mesh.devices.reshape(4, 2, 2, 8, 2), AXES)
    return jax.shard_map(
        per_device,
        mesh=mesh,
        in_specs=(
            P(SEG, HEAD),
            P(SEG, None),
            P(SEG, None),
            P(),
            P(SEG),
            P(SEG),
            P(HEAD, None, None),
            P(HEAD, SEG, None),
        ),
        out_specs=P(SEG, HEAD),
        check_vma=False,
    )
```

```python
import itertools

import jax
import jax.numpy as jnp
from jax import lax
from jax.experimental import pallas as pl
from jax.experimental.pallas import tpu as pltpu
from jax.sharding import Mesh
from jax.sharding import PartitionSpec as P

LATENT = 512
ROPE = 64
WIDTH = LATENT + ROPE
NOPE = 128
SEG_LEN = 128
VHEAD = 128
HEADS_DEV = 8
ROWS = HEADS_DEV * SEG_LEN
ANC_SEGS = 16
COLS = 448
PAD = 64

NEAR = {0: (1, 0), 1: (1, 1), 7: (0, 0), 2: (0, 1)}

NEG = -1e30
LOG2E = 1.4426950408889634
SCALE = (NOPE + ROPE) ** -0.5


AXES = ("y", "xl", "c", "z", "xh")
SEG, HEAD = AXES[:3], AXES[3:]


def seg_of(y, xl, c):
    return y * 4 + xl * 2 + c


def move(x, to):
    pairs = []
    for y, xl, c, z, xh in itertools.product(range(4), range(2), range(2), range(8), range(2)):
        ty, txl, tc, tz, txh = to(y, xl, c, z, xh)
        pairs.append((seg_of(y, xl, c) * 16 + z * 2 + xh, seg_of(ty, txl, tc) * 16 + tz * 2 + txh))
    return lax.ppermute(x, AXES, pairs)


def swap_core(x):
    return move(x, lambda y, xl, c, z, xh: (y, xl, 1 - c, z, xh))


def swap_x(x, a, b):
    return move(x, lambda y, xl, c, z, xh: (y, xl ^ a, c, z, xh ^ b))


def from_y(x, r):
    return move(x, lambda y, xl, c, z, xh: ((y - r) % 4, xl, c, z, xh))


def to_z(x, k):
    return move(x, lambda y, xl, c, z, xh: (y, xl, c, (z + k) % 8, xh))


def to_owner(x, k):
    def to(y, xl, c, z, xh):
        for half in range(2):
            owner = xl * 2 + c + 4 * half
            step = (z + k - owner) * (1 - 2 * c) % 8
            if step in NEAR:
                return (y, xl ^ NEAR[step][0], c ^ NEAR[step][1], owner, xh)

    return move(x, to)


def cut_kernel(meta, w_ref, keep_ref, other_ref):
    for c in range(2):

        @pl.when(meta[2] == c)
        def _(c=c):
            for core, ref in ((c, keep_ref), (1 - c, other_ref)):
                for xl in range(2):
                    for xh in range(2):
                        for half in range(2):
                            start = ((xl * 2 + core + 4 * half) * 2 + xh) * COLS
                            cols = slice(half * COLS, (half + 1) * COLS)
                            ref[xl, xh, :, :, cols] = w_ref[:, :, start : start + COLS]


def small_call(kernel, name, shapes, *args):
    vmem = pl.BlockSpec(memory_space=pltpu.VMEM)
    return pl.pallas_call(
        kernel,
        out_shape=[jax.ShapeDtypeStruct(x, jnp.bfloat16) for x in shapes],
        in_specs=[pl.BlockSpec(memory_space=pltpu.SMEM)] + [vmem] * (len(args) - 1),
        out_specs=[vmem] * len(shapes),
        compiler_params=pltpu.CompilerParams(vmem_limit_bytes=12 * 2**20),
        cost_estimate=pl.CostEstimate(flops=0, bytes_accessed=2 * 2**20, transcendentals=0),
        name=name,
    )(*args)


def attention_kernel(meta, q_hbm, own_ref, *refs):
    anc_refs = refs[:8]
    up_hbm, out_ref, keys, scores, top, total, accum, up_ref, q_ref, mixed, where_ref, sems = refs[8:]
    y, xl, c = meta[18], meta[19], meta[20]
    length = meta[17]
    q_copy = pltpu.make_async_copy(q_hbm, q_ref, sems.at[0])
    q_copy.start()

    for slot in range(ANC_SEGS):
        where_ref[slot] = 0

    def walk(step, current):
        @pl.when(current >= 0)
        def _():
            rel_y = lax.bitwise_and((current >> 2) - y + 4, 3)
            rel_x = lax.bitwise_xor(lax.bitwise_and(current >> 1, 1), xl)
            rel_c = lax.bitwise_xor(lax.bitwise_and(current, 1), c)
            where_ref[rel_c * 8 + rel_y * 2 + rel_x] = 1

        return jnp.where(current >= 0, meta[jnp.maximum(current, 0)], -1)

    lax.fori_loop(0, ANC_SEGS, walk, meta[16])

    keys[0, PAD : PAD + WIDTH] = own_ref[...]
    end = jnp.int32(1)
    for slot in range(ANC_SEGS):
        used = where_ref[slot]

        @pl.when(used == 1)
        def _(slot=slot, place=end):
            keys[place, PAD : PAD + WIDTH] = anc_refs[slot // 2][slot % 2]

        end = end + used
    keys[end, PAD : PAD + WIDTH] = own_ref[...]

    up_copy = pltpu.make_async_copy(up_hbm, up_ref, sems.at[1])
    up_copy.start()
    keys[:, :PAD] = jnp.zeros((ANC_SEGS + 2, PAD, SEG_LEN), jnp.bfloat16)
    keys[:, PAD + WIDTH :] = jnp.zeros((ANC_SEGS + 2, PAD, SEG_LEN), jnp.bfloat16)
    q_copy.wait()
    pairs = (end + 1) // 2

    def queries(odd):
        starts = [h * WIDTH - PAD * odd for h in range(odd, HEADS_DEV, 2)]
        return jnp.concatenate([q_ref[:, s : s + WIDTH + PAD] for s in starts], axis=0)

    def score(j):
        pair = jnp.concatenate([keys[2 * j], keys[2 * j + 1]], axis=1)
        even = jnp.dot(queries(0), pair[PAD:], preferred_element_type=jnp.float32)
        odd = jnp.dot(queries(1), pair[: WIDTH + PAD], preferred_element_type=jnp.float32)
        s = jnp.concatenate([even, odd], axis=0)
        return s[:, :SEG_LEN], s[:, SEG_LEN:]

    row = lax.broadcasted_iota(jnp.int32, (ROWS, SEG_LEN), 0) & (SEG_LEN - 1)
    col = lax.broadcasted_iota(jnp.int32, (ROWS, SEG_LEN), 1)
    left, right = score(0)
    left = jnp.where((col <= row) & (col < length), left, NEG)
    scores[0, :, :SEG_LEN] = left
    scores[0, :, SEG_LEN:] = right
    top[...] = jnp.maximum(left, right)

    def first(j, carry):
        left, right = score(j)
        right = jnp.where(2 * j + 1 < end, right, NEG)
        scores[j, :, :SEG_LEN] = left
        scores[j, :, SEG_LEN:] = right
        top[...] = jnp.maximum(top[...], jnp.maximum(left, right))
        return carry

    lax.fori_loop(1, pairs, first, 0)
    factor = SCALE * LOG2E
    high = jnp.max(top[...], axis=1, keepdims=True)
    top[...] = jnp.broadcast_to(high, (ROWS, SEG_LEN))
    total[...] = jnp.zeros_like(total)
    accum[...] = jnp.zeros_like(accum)

    def second(j, carry):
        high = top[...]
        left = jnp.exp2((scores[j, :, :SEG_LEN] - high) * factor)
        right = jnp.exp2((scores[j, :, SEG_LEN:] - high) * factor)
        total[...] += left + right
        weight = jnp.concatenate([left, right], axis=1).astype(jnp.bfloat16)
        values = pl.ds(PAD, LATENT)
        pair = jnp.concatenate([keys[2 * j, values], keys[2 * j + 1, values]], axis=1)
        accum[...] += lax.dot_general(
            weight, pair, (((1,), (1,)), ((), ())), preferred_element_type=jnp.float32
        )
        return carry

    lax.fori_loop(0, pairs, second, 0)
    up_copy.wait()
    pos = lax.broadcasted_iota(jnp.int32, (SEG_LEN, VHEAD), 0)
    for h in range(HEADS_DEV):
        at = (h % 2) * (HEADS_DEV // 2) + h // 2
        rows = slice(at * SEG_LEN, (at + 1) * SEG_LEN)
        denominator = jnp.sum(total[rows], axis=1, keepdims=True)
        latent_out = (accum[rows] / denominator).astype(jnp.bfloat16)
        head_out = jnp.dot(latent_out, up_ref[h], preferred_element_type=jnp.float32)
        head_out = jnp.where(pos < length, head_out, 0.0).astype(jnp.bfloat16)
        for block in range(4):
            rel = lax.bitwise_and(block - y + 4, 3)
            mixed[rel, :, h * 32 : (h + 1) * 32] = head_out[:, block * 32 : (block + 1) * 32]
    for copy in range(4):
        out_ref[copy] = mixed[...]


def attention(meta, q, own, anc, up):
    vmem = pl.BlockSpec(memory_space=pltpu.VMEM)
    hbm = pl.BlockSpec(memory_space=pltpu.HBM)
    return pl.pallas_call(
        attention_kernel,
        out_shape=jax.ShapeDtypeStruct((4, 4, SEG_LEN, 256), jnp.bfloat16),
        in_specs=[pl.BlockSpec(memory_space=pltpu.SMEM), hbm] + [vmem] * 9 + [hbm],
        out_specs=vmem,
        scratch_shapes=[
            pltpu.VMEM((ANC_SEGS + 2, WIDTH + 2 * PAD, SEG_LEN), jnp.bfloat16),
            pltpu.VMEM((9, ROWS, 2 * SEG_LEN), jnp.float32),
            pltpu.VMEM((ROWS, SEG_LEN), jnp.float32),
            pltpu.VMEM((ROWS, SEG_LEN), jnp.float32),
            pltpu.VMEM((ROWS, LATENT), jnp.float32),
            pltpu.VMEM((HEADS_DEV, LATENT, VHEAD), jnp.bfloat16),
            pltpu.VMEM((SEG_LEN, HEADS_DEV * WIDTH), jnp.bfloat16),
            pltpu.VMEM((4, SEG_LEN, 256), jnp.bfloat16),
            pltpu.SMEM((ANC_SEGS,), jnp.int32),
            pltpu.SemaphoreType.DMA((2,)),
        ],
        compiler_params=pltpu.CompilerParams(vmem_limit_bytes=52 * 2**20),
        cost_estimate=pl.CostEstimate(
            flops=10**6, bytes_accessed=2**16, transcendentals=0
        ),
        name="attention",
    )(meta, q, own, *anc, up)


def projected(meta, heads, weights, left, partial):
    xl, xh = meta[19], meta[22]
    w0, w1, w3, w2a, w2b = weights
    weights = [[w0.at[0], w1.at[0], w2a, w3.at[0]], [w0.at[1], w1.at[1], w2b, w3.at[1]]]
    for b in range(2):
        for a in range(2):
            source = lax.bitwise_xor(xl, a) * 2 + lax.bitwise_xor(xh, b)
            for r in range(4):
                cols = slice(b * 1024 + r * 256, b * 1024 + r * 256 + 256)
                left[a * SEG_LEN : (a + 1) * SEG_LEN, cols] = heads[source, r]
    for start in range(0, 2 * COLS, 256):
        cols = slice(start, min(start + 256, 2 * COLS))
        right = jnp.concatenate([weights[b][r][:, cols] for b in range(2) for r in range(4)], axis=0)
        value = jnp.dot(left[...], right, preferred_element_type=jnp.float32)
        for a in range(2):
            partial[a, cols] = value[a * SEG_LEN : (a + 1) * SEG_LEN].T.astype(jnp.bfloat16)


def own_kernel(meta, heads, w0, w1, w3, w2a, w2b, partial, left):
    projected(meta, heads, (w0, w1, w3, w2a, w2b), left, partial)


def other_kernel(meta, heads, w0, w1, w3, w2a, w2b, own, *refs):
    outs = refs[:6]
    partial, left = refs[6:]
    projected(meta, heads, (w0, w1, w3, w2a, w2b), left, partial)
    xl, c, z = meta[19], meta[20], meta[21]
    places = {0: (0, None), 1: (1, 0), 3: (1, 1), 7: (2, 0), 5: (2, 1), 4: (3, None), 2: (4, None), 6: (5, None)}
    for k, (out, part) in places.items():
        step = lax.bitwise_and((z + k - xl * 2 - c) * (1 - 2 * c), 7)
        upper = (step >= 3) & (step <= 6)
        near = lax.bitwise_and(jnp.where(upper, step - 4, step), 7)
        a = sum(jnp.where(near == n, x, 0) for n, (x, d) in NEAR.items())
        core = sum(jnp.where(near == n, d, 0) for n, (x, d) in NEAR.items())
        ref = outs[out] if part is None else outs[out].at[part]
        for half in range(2):
            for d, tiles in enumerate((own, partial)):

                @pl.when((upper == (half == 1)) & (core == d))
                def _(ref=ref, a=a, half=half, tiles=tiles):
                    ref[...] = tiles[a, half * COLS : (half + 1) * COLS]


def project(meta, heads, weights, own=None):
    vmem = pl.BlockSpec(memory_space=pltpu.VMEM)
    half = jax.ShapeDtypeStruct((2, 2 * COLS, SEG_LEN), jnp.bfloat16)
    one = jax.ShapeDtypeStruct((COLS, SEG_LEN), jnp.bfloat16)
    two = jax.ShapeDtypeStruct((2, COLS, SEG_LEN), jnp.bfloat16)
    left = pltpu.VMEM((2 * SEG_LEN, 2048), jnp.bfloat16)
    args = (meta, heads, *weights) if own is None else (meta, heads, *weights, own)
    return pl.pallas_call(
        own_kernel if own is None else other_kernel,
        out_shape=half if own is None else [one, two, two, one, one, one],
        in_specs=[pl.BlockSpec(memory_space=pltpu.SMEM)] + [vmem] * (len(args) - 1),
        out_specs=vmem if own is None else [vmem] * 6,
        scratch_shapes=[left] if own is None else [pltpu.VMEM(half.shape, half.dtype), left],
        compiler_params=pltpu.CompilerParams(vmem_limit_bytes=20 * 2**20),
        cost_estimate=pl.CostEstimate(flops=10**6, bytes_accessed=2**16, transcendentals=0),
        name="project_own" if own is None else "project",
    )(*args)


def per_device(
    queries,
    leaf_latent,
    ancestor_latent,
    ancestor_parent,
    leaf_parent,
    leaf_length,
    value_up,
    out_weight,
):
    y, xl, c, z, xh = [lax.axis_index(name) for name in AXES]
    place = jnp.stack([y, xl, c, z, xh]).astype(jnp.int32)
    meta = jnp.concatenate([ancestor_parent, leaf_parent, leaf_length, place])

    mine = ancestor_latent.T
    column = jnp.stack([mine, swap_x(mine, 1, 0)])

    keep, other = small_call(cut_kernel, "cut", [(2, 2, HEADS_DEV, 8, 2 * COLS)] * 2, place, out_weight)
    other = swap_core(other)
    cores = jnp.where(c == 0, jnp.stack([keep, other], 3), jnp.stack([other, keep], 3))

    def for_x(a, b):
        part = lax.dynamic_index_in_dim(cores, xl ^ a, 0, keepdims=False)
        return lax.dynamic_index_in_dim(part, xh ^ b, 0, keepdims=False)

    w00, w10, w11 = for_x(0, 0), swap_x(for_x(1, 0), 1, 0), swap_x(for_x(1, 1), 1, 1)
    w01, _ = lax.optimization_barrier((for_x(0, 1), w10))
    w01 = swap_x(w01, 0, 1)
    anc = [column] + [from_y(column, r) for r in (1, 2, 3)]
    w0, _ = lax.optimization_barrier(([[w00, w01], [w10, w11]], anc))
    anc = anc + [swap_core(x) for x in anc]

    w0 = [jnp.stack(x) for x in w0]
    w0 = jnp.where(xl == 0, jnp.stack(w0, 2), jnp.stack(w0[::-1], 2)).reshape(2, 256, 2 * COLS)
    w1, w3 = from_y(w0, 1), from_y(w0, 3)
    w2a, w2b = w1[0], w3[1]

    head_out = attention(meta, queries, leaf_latent.T, anc, value_up)

    w2a, w2b, _ = lax.optimization_barrier((w2a, w2b, head_out))
    w2a, w2b = from_y(w2a, 1), from_y(w2b, 3)
    heads = lax.all_to_all(head_out, ("xl", "xh"), 0, 0)
    heads, w2a, w2b = lax.optimization_barrier((heads, w2a, w2b))
    other = swap_core(heads)
    weights = (w0, w1, w3, w2a, w2b)
    own = project(meta, heads, weights)
    mine, right, left, far, right2, left2 = project(meta, other, weights, own)
    right, left = to_z(right, 1), to_z(left, -1)
    far = move(far, lambda y, xl, c, z, xh: (y, xl, c, (z + 2 - 4 * c) % 8, xh))

    def f32(x):
        return x.astype(jnp.float32)

    mine = f32(mine) + f32(right[0]) + f32(left[0])
    right2 = f32(right2) + f32(right[1]) + jnp.where(c == 0, f32(far), 0.0)
    left2 = f32(left2) + f32(left[1]) + jnp.where(c == 1, f32(far), 0.0)
    terms = [to_owner(x.astype(jnp.bfloat16), k) for x, k in ((mine, 0), (right2, 2), (left2, -2))]
    return (f32(terms[0]) + f32(terms[1]) + f32(terms[2])).astype(jnp.bfloat16).T


def solution(mesh):
    mesh = Mesh(mesh.devices.reshape(4, 2, 2, 8, 2), AXES)
    return jax.shard_map(
        per_device,
        mesh=mesh,
        in_specs=(
            P(SEG, HEAD),
            P(SEG, None),
            P(SEG, None),
            P(),
            P(SEG),
            P(SEG),
            P(HEAD, None, None),
            P(HEAD, SEG, None),
        ),
        out_specs=P(SEG, HEAD),
        check_vma=False,
    )
```
